32 devices in a mesh: wide: 16 (over z, y, x), narrow: 2 (over core).
Axes of the slice: x: 2, y: 2, z: 4, core: 2. Of those that a mesh axis runs over, the one named last changes fastest.
Arguments:
- integrals: bfloat16 [32, 6, 256, 1024], P(('wide', 'narrow')), may hold values from -1 to 1
- amplitudes: bfloat16 [32, 6, 256, 512], P(('wide', 'narrow')), may hold values from -6 to 6
- tile_count: int32 [32], P(('wide', 'narrow')), may hold values from 1 to 6, as said below
- row_orbitals: int32 [1024, 2], P(('wide', 'narrow')), may hold values from 0 to 575
- virtual_energy: float32 [576], replicated, may hold values from 0.2 to 3
- occupied_energy: float32 [512], replicated, may hold values from -3 to -0.8
- other_terms: float32 [1024, 512], P(('wide', 'narrow')), may hold values from -20 to 20
Outputs:
- update: float32 [1024, 512], P(('wide', 'narrow'))
- update_norm: float32 [], replicated
The draws below stay inside these ranges and needn't reach their ends.
Inputs may be any that keep to these rules, and one draw needn't show every extreme that they name: A device's screened tiles are its first tile_count slots; some device holds 6 in every draw.
All inputs are finite; a program needn't handle non-finite values.
Results may differ from the reference program's by a relative error of at most 0.0003.
Values sent between devices are 32-bit elements; how exact they have to be, the bound alone decides.
No kernel may reach another device: no remote copies, remote signals or barrier semaphores. Data moves between devices by JAX's collectives and lax.ppermute only.
A program may use at most 64 MiB of HBM per device.

```python
import math
import jax
import jax.numpy as jnp
from jax import lax

NV = 576
NO = 512
TILE = 256
ROWS = 1024
S_DEV = 6
DEVICES = 32


def draw_tile_count(key, part):
    key_base = jax.random.fold_in(key, 11)
    key_heavy = jax.random.fold_in(key, 12)
    key_peak = jax.random.fold_in(key, 13)
    base_count = jax.random.randint(key_base, (DEVICES,), 1, 3)
    heavy_mask = jax.random.randint(key_heavy, (DEVICES,), 0, 8) == 0
    peak_device = jax.random.randint(key_peak, (), 0, DEVICES)
    device_ids = jnp.arange(DEVICES, dtype=jnp.int32)
    return jnp.where(heavy_mask | (device_ids == peak_device), S_DEV, base_count).astype(jnp.int32)


def draw_integrals(key, part):
    key_noise = jax.random.fold_in(key, 21)
    key_pair = jax.random.fold_in(key, 22)
    key_mean = jax.random.fold_in(key, 23)
    weight_scale = (2.0 * TILE * DEVICES) ** (-0.5)
    mean_scale = (1.0 * TILE * DEVICES) ** (-0.5)
    pairing = jax.random.permutation(key_pair, DEVICES).astype(jnp.int32)
    row_block = (jnp.arange(ROWS, dtype=jnp.int32) // (ROWS // DEVICES)).astype(jnp.int32)
    spike = jnp.where(pairing[:, None] == row_block[None, :], 6.0, 1.0).astype(jnp.float32)
    noise = jnp.clip(jax.random.normal(key_noise, (DEVICES, S_DEV, TILE, ROWS), jnp.float32), -4.0, 4.0)
    row_mean = jax.random.uniform(key_mean, (ROWS,), jnp.float32, -1.5, 1.5)
    value = weight_scale * (noise * spike[:, None, None, :] + mean_scale * row_mean[None, None, None, :])
    return value.astype(jnp.bfloat16)


def draw_amplitudes(key, part):
    key_noise = jax.random.fold_in(key, 31)
    key_column = jax.random.fold_in(key, 32)
    noise = jnp.clip(jax.random.normal(key_noise, (DEVICES, S_DEV, TILE, NO), jnp.float32), -4.5, 4.5)
    column_offset = jax.random.uniform(key_column, (NO,), jnp.float32, -1.0, 1.0)
    return (noise + column_offset[None, None, None, :]).astype(jnp.bfloat16)


def draw_other_terms(key, part):
    row_place = (jnp.arange(ROWS, dtype=jnp.float32) / ROWS)[:, None]
    col_place = (jnp.arange(NO, dtype=jnp.float32) / NO)[None, :]
    noise = jnp.clip(jax.random.normal(key, (ROWS, NO), jnp.float32), -6.0, 6.0)
    scale = 0.3 * jnp.power(10.0, 0.5 * row_place + 0.5 * col_place)
    return (noise * scale).astype(jnp.float32)


def with_ends(entries, stream_key, low, high):
    extent = entries.shape
    spot = [jax.random.randint(jax.random.fold_in(stream_key, axis), (), 0, extent[axis]) for axis in range(len(extent))]
    entries = entries.at[tuple(spot)].set(low)
    longest = extent.index(max(extent))
    spot[longest] = (spot[longest] + 1) % extent[longest]
    return entries.at[tuple(spot)].set(high)


def setup_inputs(seed: int = 0) -> dict:
    splits = jax.random.split(jax.random.key(seed), 8)
    return {
        "integrals": draw_integrals(jax.random.fold_in(splits[7], 71), 0),
        "amplitudes": draw_amplitudes(jax.random.fold_in(splits[7], 71), 0),
        "tile_count": draw_tile_count(jax.random.fold_in(splits[7], 71), 0),
        "row_orbitals": with_ends(jax.random.randint(splits[3], (ROWS, 2), 0, NV), jax.random.fold_in(splits[3], 1), 0, NV - 1).astype(jnp.int32),
        "virtual_energy": jnp.clip(jnp.exp(jax.random.uniform(splits[4], (NV,), jnp.float32, math.log(0.2), math.log(3.0))), 0.2, 3.0),
        "occupied_energy": jnp.clip(jax.random.uniform(splits[5], (NO,), jnp.float32, -3.0, -0.8), -3.0, -0.8),
        "other_terms": draw_other_terms(jax.random.fold_in(splits[7], 71), 0),
    }


def reference(integrals, amplitudes, tile_count, row_orbitals, virtual_energy, occupied_energy, other_terms):

    def device_step(running, items):
        tile_block, amp_rows, live_count = items

        def add_tile(slot_index, partial_value):
            tile_one = lax.dynamic_index_in_dim(tile_block, slot_index, 0, keepdims=False)
            amp_one = lax.dynamic_index_in_dim(amp_rows, slot_index, 0, keepdims=False)
            return partial_value + lax.dot_general(tile_one, amp_one, (((0,), (0,)), ((), ())), preferred_element_type=jnp.float32)
        return (lax.fori_loop(jnp.int32(0), live_count, add_tile, running), None)
    ladder, _ = lax.scan(device_step, jnp.zeros((ROWS, NO), jnp.float32), (integrals, amplitudes, tile_count))
    first_energy = virtual_energy[row_orbitals[:, 0]]
    second_energy = virtual_energy[row_orbitals[:, 1]]
    denominator = occupied_energy[None, :] - (first_energy + second_energy)[:, None]
    update = (ladder + other_terms) / denominator
    update_norm = jnp.sqrt(jnp.sum(update * update) / (ROWS * NO))
    return (update, update_norm)
```

```python
import functools
import jax
import jax.numpy as jnp
from jax import lax
from jax.experimental import pallas as pl
from jax.experimental.pallas import tpu as pltpu
from jax.sharding import PartitionSpec as P

AXES = ("wide", "narrow")
GROUPS = 3
ROW_CHUNK = 256


def bit_order(stream, wide_bits):
    low = list(range(wide_bits))
    if wide_bits >= 2 and stream == 1:
        low[0], low[1] = low[1], low[0]
    return low


def ladder_kernel(block_rows, orders, place_ref, count_ref, tiles_ref, amps_ref, *refs):
    streams = len(orders)
    outs = refs[:streams]
    tile_buf, amp_buf, total, tile_sem, amp_sem = refs[streams:]
    slots, _, rows = tile_buf.shape
    width = amp_buf.shape[2]
    part = width // streams
    live = count_ref[0]
    wide_me, narrow_me = place_ref[0], place_ref[1]

    def copies(slot):
        return (
            pltpu.make_async_copy(amps_ref.at[slot], amp_buf.at[slot], amp_sem.at[slot]),
            pltpu.make_async_copy(tiles_ref.at[slot], tile_buf.at[slot], tile_sem.at[slot]),
        )

    for slot in range(slots):
        for copy in copies(slot):
            copy.start()
    group = slots // GROUPS
    for first in range(0, slots, group):
        members = range(first, first + group)
        for slot in members:
            for copy in copies(slot):
                copy.wait()
        amps = jnp.concatenate(
            [jnp.where(slot < live, amp_buf[slot], jnp.zeros_like(amp_buf[slot])) for slot in members], 0
        )
        for start in range(0, rows, ROW_CHUNK):
            tiles = jnp.concatenate([tile_buf[slot, :, start : start + ROW_CHUNK] for slot in members], 0)
            term = lax.dot_general(tiles, amps, (((0,), (0,)), ((), ())), preferred_element_type=jnp.float32)
            if first:
                term += total[start : start + ROW_CHUNK]
            if first + group < slots:
                total[start : start + ROW_CHUNK] = term
                continue
            for offset in range(0, ROW_CHUNK, block_rows):
                owner = (start + offset) // block_rows
                apart = (owner // 2) ^ wide_me
                cross = (owner % 2) ^ narrow_me
                for stream, order in enumerate(orders):
                    spot = cross
                    for bit in order:
                        spot = spot * 2 + ((apart >> bit) & 1)
                    where = pl.ds(pl.multiple_of(spot * block_rows, block_rows), block_rows)
                    outs[stream][where, :] = term[offset : offset + block_rows, stream * part : (stream + 1) * part]


def flip(value, axis, size, bits):
    return lax.ppermute(value, axis, [(i, i ^ bits) for i in range(size)])


def fast_ladder(tile_block, amp_rows, tile_count, wide, narrow):
    slots, depth, rows = tile_block.shape
    width = amp_rows.shape[2]
    block_rows = rows // (wide * narrow)
    wide_bits = wide.bit_length() - 1
    orders = [bit_order(stream, wide_bits) for stream in range(2)]
    part = width // 2
    place = jnp.stack([lax.axis_index("wide"), lax.axis_index("narrow")]).astype(jnp.int32)
    streams = pl.pallas_call(
        functools.partial(ladder_kernel, block_rows, orders),
        out_shape=[jax.ShapeDtypeStruct((rows, part), jnp.float32)] * 2,
        in_specs=[pl.BlockSpec(memory_space=pltpu.SMEM)] * 2 + [pl.BlockSpec(memory_space=pltpu.HBM)] * 2,
        out_specs=[pl.BlockSpec(memory_space=pltpu.VMEM)] * 2,
        scratch_shapes=[
            pltpu.VMEM((slots, depth, rows), tile_block.dtype),
            pltpu.VMEM((slots, depth, width), amp_rows.dtype),
            pltpu.VMEM((rows, width), jnp.float32),
            pltpu.SemaphoreType.DMA((slots,)),
            pltpu.SemaphoreType.DMA((slots,)),
        ],
        compiler_params=pltpu.CompilerParams(vmem_limit_bytes=32 << 20),
        cost_estimate=pl.CostEstimate(
            flops=2 * slots * depth * rows * width,
            bytes_accessed=2 * slots * depth * (rows + width) + 4 * rows * width,
            transcendentals=0,
        ),
    )(place, tile_count, tile_block, amp_rows)
    half = rows // 2
    streams = [s[:half] + flip(s[half:], "narrow", narrow, 1) for s in streams]
    for step in range(2):
        half //= 2
        streams = [
            s[:half] + flip(s[half:], "wide", wide, 1 << order[step]) for s, order in zip(streams, orders)
        ]
    joined = jnp.concatenate(streams, axis=1)
    ladder = joined[:block_rows]
    rest = orders[0][2:]
    for spot in range(1, 1 << len(rest)):
        bits = 0
        for index, bit in enumerate(rest):
            if (spot >> (len(rest) - 1 - index)) & 1:
                bits |= 1 << bit
        ladder += flip(joined[spot * block_rows : (spot + 1) * block_rows], "wide", wide, bits)
    return ladder


def plain_ladder(tile_block, amp_rows, tile_count):
    slots, depth, rows = tile_block.shape
    live = lax.broadcasted_iota(jnp.int32, (slots, 1, 1), 0) < tile_count[0]
    amps = jnp.where(live, amp_rows, jnp.zeros_like(amp_rows))
    partial = lax.dot_general(
        tile_block.reshape(slots * depth, rows),
        amps.reshape(slots * depth, amp_rows.shape[2]),
        (((0,), (0,)), ((), ())),
        preferred_element_type=jnp.float32,
    )
    partial = lax.psum_scatter(partial, "wide", scatter_dimension=0, tiled=True)
    return lax.psum_scatter(partial, "narrow", scatter_dimension=0, tiled=True)


def shards(wide, narrow, integrals, amplitudes, tile_count, row_orbitals, virtual_energy, occupied_energy, other_terms):
    tile_block = integrals[0]
    amp_rows = amplitudes[0]
    rows = tile_block.shape[2]
    width = amp_rows.shape[2]
    devices = wide * narrow
    fast = narrow == 2 and wide >= 4 and wide & (wide - 1) == 0 and rows % (16 * devices) == 0
    if fast:
        ladder = fast_ladder(tile_block, amp_rows, tile_count, wide, narrow)
    else:
        ladder = plain_ladder(tile_block, amp_rows, tile_count)
    orbital_ids = lax.broadcasted_iota(jnp.int32, (1, virtual_energy.shape[0]), 1)
    energy_row = virtual_energy[None, :]
    first_energy = jnp.sum(jnp.where(row_orbitals[:, 0:1] == orbital_ids, energy_row, 0.0), axis=1)
    second_energy = jnp.sum(jnp.where(row_orbitals[:, 1:2] == orbital_ids, energy_row, 0.0), axis=1)
    denominator = occupied_energy[None, :] - (first_energy + second_energy)[:, None]
    update = (ladder + other_terms) / denominator
    square = jnp.sum(update * update)
    if fast:
        every = lax.all_to_all(jnp.full((devices, 128), square), AXES, 0, 0, tiled=True)
        square_total = jnp.sum(every[:, 0])
    else:
        square_total = lax.psum(square, AXES)
    update_norm = jnp.sqrt(square_total / (rows * width))
    return (update, update_norm)


def solution(mesh):
    in_specs = (P(AXES, None, None, None), P(AXES, None, None, None), P(AXES), P(AXES, None), P(), P(), P(AXES, None))
    out_specs = (P(AXES, None), P())
    body = functools.partial(shards, mesh.shape["wide"], mesh.shape["narrow"])
    return jax.shard_map(body, mesh=mesh, in_specs=in_specs, out_specs=out_specs, check_vma=False)
```

```python
import functools
import jax
import jax.numpy as jnp
from jax import lax
from jax.experimental import pallas as pl
from jax.experimental.pallas import tpu as pltpu
from jax.sharding import PartitionSpec as P

AXES = ("wide", "narrow")
ROW_CHUNK = 256
PLAN = ((0, 2, (0, 1), (1, 0)), (2, 4, (0, 1), (1, 0)))
SPOTS = (3, 2, 1)
STATIC = False


def ladder_kernel(block_rows, orders, bounds, place_ref, count_ref, tiles_ref, amps_ref, *refs):
    outs = refs[: len(bounds)]
    tile_buf, amp_buf, total, tile_sem, amp_sem = refs[len(bounds) :]
    slots, _, rows = tile_buf.shape
    live = count_ref[0]
    wide_me, narrow_me = place_ref[0], place_ref[1]

    def copies(slot):
        return (
            pltpu.make_async_copy(amps_ref.at[slot], amp_buf.at[slot], amp_sem.at[slot]),
            pltpu.make_async_copy(tiles_ref.at[slot], tile_buf.at[slot], tile_sem.at[slot]),
        )

    for slot in range(slots):

        def load_slot(slot=slot):
            for copy in copies(slot):
                copy.start()

        if slot and not STATIC:
            pl.when(slot < live)(load_slot)
        else:
            load_slot()
    def store(start, term, fresh):
        for offset in range(0, ROW_CHUNK, block_rows):
            owner = (start + offset) // block_rows
            apart = (owner // 2) ^ wide_me
            for piece, (low, high) in enumerate(bounds):
                spot = (owner % 2) ^ narrow_me
                for bit in orders[owner % 2][piece]:
                    spot = spot * 2 + ((apart >> bit) & 1)
                where = pl.ds(pl.multiple_of(spot * block_rows, block_rows), block_rows)
                block = term[offset : offset + block_rows, low:high]
                outs[piece][where, :] = block if fresh else outs[piece][where, :] + block

    if STATIC:
        group = 2
        for first in range(0, slots, group):
            members = range(first, first + group)
            for slot in members:
                for copy in copies(slot):
                    copy.wait()
            amps = jnp.concatenate(
                [jnp.where(slot < live, amp_buf[slot], jnp.zeros_like(amp_buf[slot])) for slot in members], 0
            )
            for start in range(0, rows, ROW_CHUNK):
                tiles = jnp.concatenate([tile_buf[slot, :, start : start + ROW_CHUNK] for slot in members], 0)
                term = lax.dot_general(tiles, amps, (((0,), (0,)), ((), ())), preferred_element_type=jnp.float32)
                if first:
                    term += total[start : start + ROW_CHUNK]
                if first + group < slots:
                    total[start : start + ROW_CHUNK] = term
                else:
                    store(start, term, True)
        return
    for slot in range(slots):

        def add_slot(slot=slot):
            for copy in copies(slot):
                copy.wait()
            for start in range(0, rows, ROW_CHUNK):
                term = lax.dot_general(
                    tile_buf[slot, :, start : start + ROW_CHUNK],
                    amp_buf[slot],
                    (((0,), (0,)), ((), ())),
                    preferred_element_type=jnp.float32,
                )
                store(start, term, slot == 0)

        if slot:
            pl.when(slot < live)(add_slot)
        else:
            add_slot()


def update_kernel(count, *refs):
    parts = refs[:count]
    other_ref, energy_ref, occupied_ref, update_ref, square_ref = refs[count:]
    ladder = parts[0][...]
    for part in parts[1:]:
        ladder += part[...]
    update = (ladder + other_ref[...]) / (occupied_ref[...] - energy_ref[...])
    update_ref[...] = update
    square_ref[...] = jnp.full(square_ref.shape, jnp.sum(update * update))


def norm_kernel(entries, squares_ref, norm_ref):
    total = jnp.sum(squares_ref[...], axis=0, keepdims=True)
    norm_ref[...] = jnp.sqrt(total / entries)[:, :1]


def flip(value, devices, masks):
    pairs = [(i, i ^ (2 * masks[i % 2])) for i in range(devices)]
    return lax.ppermute(value, AXES, pairs)


def fast_ladder(tile_block, amp_rows, tile_count, wide, narrow):
    slots, depth, rows = tile_block.shape
    width = amp_rows.shape[2]
    devices = wide * narrow
    block_rows = rows // devices
    rest = tuple(range(2, wide.bit_length() - 1))
    orders = [[plan[2 + core] + rest for plan in PLAN] for core in range(2)]
    bounds = [(plan[0] * width // 4, plan[1] * width // 4) for plan in PLAN]
    place = jnp.stack([lax.axis_index("wide"), lax.axis_index("narrow")]).astype(jnp.int32)
    pieces = pl.pallas_call(
        functools.partial(ladder_kernel, block_rows, orders, bounds),
        out_shape=[pltpu.VMEM((rows, high - low), jnp.float32) for low, high in bounds],
        in_specs=[pl.BlockSpec(memory_space=pltpu.SMEM)] * 2 + [pl.BlockSpec(memory_space=pltpu.HBM)] * 2,
        out_specs=[pl.BlockSpec(memory_space=pltpu.VMEM)] * len(bounds),
        scratch_shapes=[
            pltpu.VMEM((slots, depth, rows), tile_block.dtype),
            pltpu.VMEM((slots, depth, width), amp_rows.dtype),
            pltpu.VMEM((rows, width), jnp.float32),
            pltpu.SemaphoreType.DMA((slots,)),
            pltpu.SemaphoreType.DMA((slots,)),
        ],
        compiler_params=pltpu.CompilerParams(vmem_limit_bytes=32 << 20),
    )(
        place,
        tile_count,
        pltpu.with_memory_space_constraint(tile_block, pltpu.HBM),
        pltpu.with_memory_space_constraint(amp_rows, pltpu.HBM),
    )
    half = rows // 2
    swap = [(i, i ^ 1) for i in range(devices)]
    pieces = [s[:half] + lax.ppermute(s[half:], AXES, swap) for s in pieces]
    for step in range(2):
        half //= 2
        masks = [[1 << order[piece][step] for order in orders] for piece in range(len(pieces))]
        pieces = [s[:half] + flip(s[half:], devices, mask) for s, mask in zip(pieces, masks)]
    joined = jnp.concatenate(pieces, axis=1)
    parts = [joined[:block_rows]]
    for spot in SPOTS:
        mask = sum(1 << bit for i, bit in enumerate(rest) if (spot >> (len(rest) - 1 - i)) & 1)
        parts.append(flip(joined[spot * block_rows : (spot + 1) * block_rows], devices, [mask] * 2))
    return parts


def plain_ladder(tile_block, amp_rows, tile_count):
    slots, depth, rows = tile_block.shape
    live = lax.broadcasted_iota(jnp.int32, (slots, 1, 1), 0) < tile_count[0]
    amps = jnp.where(live, amp_rows, jnp.zeros_like(amp_rows))
    partial = lax.dot_general(
        tile_block.reshape(slots * depth, rows),
        amps.reshape(slots * depth, amp_rows.shape[2]),
        (((0,), (0,)), ((), ())),
        preferred_element_type=jnp.float32,
    )
    partial = lax.psum_scatter(partial, "wide", scatter_dimension=0, tiled=True)
    return lax.psum_scatter(partial, "narrow", scatter_dimension=0, tiled=True)


def shards(wide, narrow, integrals, amplitudes, tile_count, row_orbitals, virtual_energy, occupied_energy, other_terms):
    tile_block = integrals[0]
    amp_rows = amplitudes[0]
    rows = tile_block.shape[2]
    width = amp_rows.shape[2]
    devices = wide * narrow
    fast = narrow == 2 and wide >= 16 and wide & (wide - 1) == 0 and rows % (16 * devices) == 0 and width % 512 == 0
    orbital_ids = lax.broadcasted_iota(jnp.int32, (1, virtual_energy.shape[0]), 1)
    energy_row = virtual_energy[None, :]
    first_energy = jnp.sum(jnp.where(row_orbitals[:, 0:1] == orbital_ids, energy_row, 0.0), axis=1)
    second_energy = jnp.sum(jnp.where(row_orbitals[:, 1:2] == orbital_ids, energy_row, 0.0), axis=1)
    virtual_sum = (first_energy + second_energy)[:, None]
    occupied = occupied_energy[None, :]
    if fast:
        parts = fast_ladder(tile_block, amp_rows, tile_count, wide, narrow)
        update, squares = pl.pallas_call(
            functools.partial(update_kernel, len(parts)),
            out_shape=[
                jax.ShapeDtypeStruct(other_terms.shape, jnp.float32),
                pltpu.VMEM((devices, 128), jnp.float32),
            ],
            compiler_params=pltpu.CompilerParams(vmem_limit_bytes=4 << 20),
        )(*parts, other_terms, virtual_sum, occupied)
        squares = lax.all_to_all(squares, AXES, 0, 0, tiled=True)
        update_norm = pl.pallas_call(
            functools.partial(norm_kernel, rows * width),
            out_shape=jax.ShapeDtypeStruct((1, 1), jnp.float32),
            compiler_params=pltpu.CompilerParams(vmem_limit_bytes=4 << 20),
        )(squares).reshape(())
    else:
        ladder = plain_ladder(tile_block, amp_rows, tile_count)
        update = (ladder + other_terms) / (occupied - virtual_sum)
        update_norm = jnp.sqrt(lax.psum(jnp.sum(update * update), AXES) / (rows * width))
    return (update, update_norm)


def solution(mesh):
    in_specs = (P(AXES, None, None, None), P(AXES, None, None, None), P(AXES), P(AXES, None), P(), P(), P(AXES, None))
    out_specs = (P(AXES, None), P())
    body = functools.partial(shards, mesh.shape["wide"], mesh.shape["narrow"])
    return jax.shard_map(body, mesh=mesh, in_specs=in_specs, out_specs=out_specs, check_vma=False)
```

```python
import functools
import jax
import jax.numpy as jnp
from jax import lax
from jax.experimental import pallas as pl
from jax.experimental.pallas import tpu as pltpu
from jax.sharding import PartitionSpec as P

AXES = ("wide", "narrow")
ROW_CHUNK = 256
ROUTES = ((0, 1), (1, 0))


def position(order, wide_index):
    spot = wide_index * 0
    for bit in order:
        spot = spot * 2 + ((wide_index >> bit) & 1)
    return spot


def ladder_kernel(block_rows, place_ref, count_ref, tiles_ref, amps_ref, out_ref, tile_buf, amp_buf, tile_sem, amp_sem):
    slots, _, rows = tile_buf.shape
    live = count_ref[0]
    wide_me, narrow_me = place_ref[0], place_ref[1]

    def copies(slot):
        return (
            pltpu.make_async_copy(amps_ref.at[slot], amp_buf.at[slot], amp_sem.at[slot]),
            pltpu.make_async_copy(tiles_ref.at[slot], tile_buf.at[slot], tile_sem.at[slot]),
        )

    for slot in range(slots):

        def load_slot(slot=slot):
            for copy in copies(slot):
                copy.start()

        pl.when(slot < live)(load_slot)

    def spot_of(wide, narrow, route):
        return (wide >> 2) * 8 + narrow * 4 + position(route, wide & 3)

    mine = [spot_of(wide_me, narrow_me, route) for route in ROUTES]

    def add_slots(members, fresh):
        for slot in members:
            for copy in copies(slot):
                copy.wait()
        amps = jnp.concatenate([amp_buf[slot] for slot in members], 0)
        for start in range(0, rows, ROW_CHUNK):
            tiles = jnp.concatenate([tile_buf[slot, :, start : start + ROW_CHUNK] for slot in members], 0)
            term = lax.dot_general(tiles, amps, (((0,), (0,)), ((), ())), preferred_element_type=jnp.float32)
            for offset in range(0, ROW_CHUNK, block_rows):
                wide, narrow = divmod((start + offset) // block_rows, 2)
                spot = mine[narrow] ^ spot_of(wide, narrow, ROUTES[narrow])
                where = pl.ds(pl.multiple_of(spot * block_rows, block_rows), block_rows)
                block = term[offset : offset + block_rows]
                out_ref[where, :] = block if fresh else out_ref[where, :] + block

    for first in range(0, slots, 2):
        alone = (live == first + 1) if first + 1 < slots else (live > first)
        pl.when(alone)(functools.partial(add_slots, [first], first == 0))
        if first + 1 < slots:
            pl.when(live > first + 1)(functools.partial(add_slots, [first, first + 1], first == 0))


def update_kernel(count, *refs):
    parts = refs[:count]
    other_ref, energy_ref, occupied_ref, update_ref, square_ref = refs[count:]
    ladder = parts[0][...]
    for part in parts[1:]:
        ladder += part[...]
    update = (ladder + other_ref[...]) / (occupied_ref[...] - energy_ref[...])
    update_ref[...] = update
    square_ref[...] = jnp.full(square_ref.shape, jnp.sum(update * update))


def norm_kernel(entries, squares_ref, norm_ref):
    total = jnp.sum(squares_ref[...], axis=0, keepdims=True)
    norm_ref[...] = jnp.sqrt(total / entries)[:, :1]


def flip(value, devices, masks):
    pairs = [(i, i ^ (2 * masks[i % 2])) for i in range(devices)]
    return lax.ppermute(value, AXES, pairs)


def fast_ladder(tile_block, amp_rows, tile_count, wide, narrow):
    slots, depth, rows = tile_block.shape
    width = amp_rows.shape[2]
    devices = wide * narrow
    block_rows = rows // devices
    place = jnp.stack([lax.axis_index("wide"), lax.axis_index("narrow")]).astype(jnp.int32)
    partial = pl.pallas_call(
        functools.partial(ladder_kernel, block_rows),
        out_shape=pltpu.VMEM((rows, width), jnp.float32),
        in_specs=[pl.BlockSpec(memory_space=pltpu.SMEM)] * 2 + [pl.BlockSpec(memory_space=pltpu.HBM)] * 2,
        out_specs=pl.BlockSpec(memory_space=pltpu.VMEM),
        scratch_shapes=[
            pltpu.VMEM((slots, depth, rows), tile_block.dtype),
            pltpu.VMEM((slots, depth, width), amp_rows.dtype),
            pltpu.SemaphoreType.DMA((slots,)),
            pltpu.SemaphoreType.DMA((slots,)),
        ],
        compiler_params=pltpu.CompilerParams(vmem_limit_bytes=32 << 20),
    )(
        place,
        tile_count,
        pltpu.with_memory_space_constraint(tile_block, pltpu.HBM),
        pltpu.with_memory_space_constraint(amp_rows, pltpu.HBM),
    )
    far = wide // 4
    partial = partial.reshape(far, 2, 4, block_rows, width)
    swap = [(i, i ^ 1) for i in range(devices)]
    groups = [range(far // 2), range(far // 2, far)]
    pieces = [partial[g.start : g.stop] for g in groups]
    pieces = [s[:, 0] + lax.ppermute(s[:, 1], AXES, swap) for s in pieces]
    for step in range(2):
        half = 2 >> step
        masks = [1 << route[step] for route in ROUTES]
        pieces = [s[:, :half] + flip(s[:, half:], devices, masks) for s in pieces]
    parts = []
    for g, s in zip(groups, pieces):
        for spot in g:
            block = s[spot - g.start, 0]
            parts.append(flip(block, devices, [4 * spot] * 2) if spot else block)
    return parts


def plain_ladder(tile_block, amp_rows, tile_count):
    slots, depth, rows = tile_block.shape
    live = lax.broadcasted_iota(jnp.int32, (slots, 1, 1), 0) < tile_count[0]
    amps = jnp.where(live, amp_rows, jnp.zeros_like(amp_rows))
    partial = lax.dot_general(
        tile_block.reshape(slots * depth, rows),
        amps.reshape(slots * depth, amp_rows.shape[2]),
        (((0,), (0,)), ((), ())),
        preferred_element_type=jnp.float32,
    )
    partial = lax.psum_scatter(partial, "wide", scatter_dimension=0, tiled=True)
    return lax.psum_scatter(partial, "narrow", scatter_dimension=0, tiled=True)


def shards(wide, narrow, integrals, amplitudes, tile_count, row_orbitals, virtual_energy, occupied_energy, other_terms):
    tile_block = integrals[0]
    amp_rows = amplitudes[0]
    rows = tile_block.shape[2]
    width = amp_rows.shape[2]
    devices = wide * narrow
    fast = narrow == 2 and wide >= 16 and wide & (wide - 1) == 0 and rows % (16 * devices) == 0 and width % 512 == 0
    orbital_ids = lax.broadcasted_iota(jnp.int32, (1, virtual_energy.shape[0]), 1)
    energy_row = virtual_energy[None, :]
    first_energy = jnp.sum(jnp.where(row_orbitals[:, 0:1] == orbital_ids, energy_row, 0.0), axis=1)
    second_energy = jnp.sum(jnp.where(row_orbitals[:, 1:2] == orbital_ids, energy_row, 0.0), axis=1)
    virtual_sum = (first_energy + second_energy)[:, None]
    occupied = occupied_energy[None, :]
    if fast:
        parts = fast_ladder(tile_block, amp_rows, tile_count, wide, narrow)
        update, squares = pl.pallas_call(
            functools.partial(update_kernel, len(parts)),
            out_shape=[
                jax.ShapeDtypeStruct(other_terms.shape, jnp.float32),
                pltpu.VMEM((devices, 128), jnp.float32),
            ],
            compiler_params=pltpu.CompilerParams(vmem_limit_bytes=4 << 20),
        )(*parts, other_terms, virtual_sum, occupied)
        squares = lax.all_to_all(squares, AXES, 0, 0, tiled=True)
        update_norm = pl.pallas_call(
            functools.partial(norm_kernel, rows * width),
            out_shape=jax.ShapeDtypeStruct((1, 1), jnp.float32),
            compiler_params=pltpu.CompilerParams(vmem_limit_bytes=4 << 20),
        )(squares).reshape(())
    else:
        ladder = plain_ladder(tile_block, amp_rows, tile_count)
        update = (ladder + other_terms) / (occupied - virtual_sum)
        update_norm = jnp.sqrt(lax.psum(jnp.sum(update * update), AXES) / (rows * width))
    return (update, update_norm)


def solution(mesh):
    in_specs = (P(AXES, None, None, None), P(AXES, None, None, None), P(AXES), P(AXES, None), P(), P(), P(AXES, None))
    out_specs = (P(AXES, None), P())
    body = functools.partial(shards, mesh.shape["wide"], mesh.shape["narrow"])
    return jax.shard_map(body, mesh=mesh, in_specs=in_specs, out_specs=out_specs, check_vma=False)
```

```python
import functools
import jax
import jax.numpy as jnp
from jax import lax
from jax.experimental import pallas as pl
from jax.experimental.pallas import tpu as pltpu
from jax.sharding import PartitionSpec as P

AXES = ("wide", "narrow")
ROW_CHUNK = 256
FAR_ROUTES = ((0, 1), (1, 0))
NEAR_ROUTES = ((2, 1, 0), (1, 0, 2))


def position(order, wide_index):
    spot = wide_index * 0
    for bit in order:
        spot = spot * 2 + ((wide_index >> bit) & 1)
    return spot


def ladder_kernel(block_rows, planes, place_ref, count_ref, tiles_ref, amps_ref, out_ref, tile_buf, amp_buf, tile_sem, amp_sem):
    slots, _, rows = tile_buf.shape
    live = count_ref[0]
    wide_me, narrow_me = place_ref[0], place_ref[1]

    def copies(slot):
        return (
            pltpu.make_async_copy(amps_ref.at[slot], amp_buf.at[slot], amp_sem.at[slot]),
            pltpu.make_async_copy(tiles_ref.at[slot], tile_buf.at[slot], tile_sem.at[slot]),
        )

    for slot in range(slots):

        def load_slot(slot=slot):
            for copy in copies(slot):
                copy.start()

        pl.when(slot < live)(load_slot)

    def spot_of(wide_index, narrow):
        apart = wide_me ^ wide_index
        cross = narrow_me ^ narrow
        plane = apart >> 2
        first, second, third = NEAR_ROUTES[narrow]
        far_spot = plane * 8 + cross * 4 + position(FAR_ROUTES[narrow], apart)
        near_spot = (plane >> 1) * 16 + position((third,), apart) * 8 + cross * 4 + position((first, second), apart)
        return jnp.where(plane >= planes // 2, far_spot, near_spot)

    def add_slots(members, fresh):
        for slot in members:
            for copy in copies(slot):
                copy.wait()
        amps = jnp.concatenate([amp_buf[slot] for slot in members], 0)
        for start in range(0, rows, ROW_CHUNK):
            tiles = jnp.concatenate([tile_buf[slot, :, start : start + ROW_CHUNK] for slot in members], 0)
            term = lax.dot_general(tiles, amps, (((0,), (0,)), ((), ())), preferred_element_type=jnp.float32)
            for offset in range(0, ROW_CHUNK, block_rows):
                wide, narrow = divmod((start + offset) // block_rows, 2)
                spot = spot_of(wide, narrow)
                where = pl.ds(pl.multiple_of(spot * block_rows, block_rows), block_rows)
                block = term[offset : offset + block_rows]
                out_ref[where, :] = block if fresh else out_ref[where, :] + block

    for first in range(0, slots, 2):
        alone = (live == first + 1) if first + 1 < slots else (live > first)
        pl.when(alone)(functools.partial(add_slots, [first], first == 0))
        if first + 1 < slots:
            pl.when(live > first + 1)(functools.partial(add_slots, [first, first + 1], first == 0))


def update_kernel(count, *refs):
    parts = refs[:count]
    other_ref, energy_ref, occupied_ref, update_ref, square_ref = refs[count:]
    ladder = parts[0][...]
    for part in parts[1:]:
        ladder += part[...]
    update = (ladder + other_ref[...]) / (occupied_ref[...] - energy_ref[...])
    update_ref[...] = update
    square_ref[...] = jnp.full(square_ref.shape, jnp.sum(update * update))


def norm_kernel(entries, squares_ref, norm_ref):
    total = jnp.sum(squares_ref[...], axis=0, keepdims=True)
    norm_ref[...] = jnp.sqrt(total / entries)[:, :1]


def flip(value, devices, masks):
    pairs = [(i, i ^ (2 * masks[i % 2])) for i in range(devices)]
    return lax.ppermute(value, AXES, pairs)


def fast_ladder(tile_block, amp_rows, tile_count, wide, narrow):
    slots, depth, rows = tile_block.shape
    width = amp_rows.shape[2]
    devices = wide * narrow
    block_rows = rows // devices
    place = jnp.stack([lax.axis_index("wide"), lax.axis_index("narrow")]).astype(jnp.int32)
    partial = pl.pallas_call(
        functools.partial(ladder_kernel, block_rows, wide // 4),
        out_shape=pltpu.VMEM((rows, width), jnp.float32),
        in_specs=[pl.BlockSpec(memory_space=pltpu.SMEM)] * 2 + [pl.BlockSpec(memory_space=pltpu.HBM)] * 2,
        out_specs=pl.BlockSpec(memory_space=pltpu.VMEM),
        scratch_shapes=[
            pltpu.VMEM((slots, depth, rows), tile_block.dtype),
            pltpu.VMEM((slots, depth, width), amp_rows.dtype),
            pltpu.SemaphoreType.DMA((slots,)),
            pltpu.SemaphoreType.DMA((slots,)),
        ],
        compiler_params=pltpu.CompilerParams(vmem_limit_bytes=32 << 20),
    )(
        place,
        tile_count,
        pltpu.with_memory_space_constraint(tile_block, pltpu.HBM),
        pltpu.with_memory_space_constraint(amp_rows, pltpu.HBM),
    )
    far = wide // 4
    partial = partial.reshape(far, 2, 4, block_rows, width)
    swap = [(i, i ^ 1) for i in range(devices)]
    groups = [range(far // 2), range(far // 2, far)]
    pieces = [partial[g.start : g.stop] for g in groups]
    pieces = [s[:, 0] + lax.ppermute(s[:, 1], AXES, swap) for s in pieces]
    for step in range(2):
        half = 2 >> step
        masks = [[1 << route[step] for route in routes] for routes in (NEAR_ROUTES, FAR_ROUTES)]
        pieces = [s[:, :half] + flip(s[:, half:], devices, mask) for s, mask in zip(pieces, masks)]
    parts = []
    for g, s in zip(groups, pieces):
        for spot in g:
            block = s[spot - g.start, 0]
            masks = [4 * spot] * 2
            if spot < far // 2:
                masks = [(4 * spot & ~4) | ((spot & 1) << route[2]) for route in NEAR_ROUTES]
            parts.append(flip(block, devices, masks) if spot else block)
    return parts


def plain_ladder(tile_block, amp_rows, tile_count):
    slots, depth, rows = tile_block.shape
    live = lax.broadcasted_iota(jnp.int32, (slots, 1, 1), 0) < tile_count[0]
    amps = jnp.where(live, amp_rows, jnp.zeros_like(amp_rows))
    partial = lax.dot_general(
        tile_block.reshape(slots * depth, rows),
        amps.reshape(slots * depth, amp_rows.shape[2]),
        (((0,), (0,)), ((), ())),
        preferred_element_type=jnp.float32,
    )
    partial = lax.psum_scatter(partial, "wide", scatter_dimension=0, tiled=True)
    return lax.psum_scatter(partial, "narrow", scatter_dimension=0, tiled=True)


def shards(wide, narrow, integrals, amplitudes, tile_count, row_orbitals, virtual_energy, occupied_energy, other_terms):
    tile_block = integrals[0]
    amp_rows = amplitudes[0]
    rows = tile_block.shape[2]
    width = amp_rows.shape[2]
    devices = wide * narrow
    fast = narrow == 2 and wide >= 16 and wide & (wide - 1) == 0 and rows % (16 * devices) == 0 and width % 512 == 0
    orbital_ids = lax.broadcasted_iota(jnp.int32, (1, virtual_energy.shape[0]), 1)
    energy_row = virtual_energy[None, :]
    first_energy = jnp.sum(jnp.where(row_orbitals[:, 0:1] == orbital_ids, energy_row, 0.0), axis=1)
    second_energy = jnp.sum(jnp.where(row_orbitals[:, 1:2] == orbital_ids, energy_row, 0.0), axis=1)
    virtual_sum = (first_energy + second_energy)[:, None]
    occupied = occupied_energy[None, :]
    if fast:
        parts = fast_ladder(tile_block, amp_rows, tile_count, wide, narrow)
        update, squares = pl.pallas_call(
            functools.partial(update_kernel, len(parts)),
            out_shape=[
                jax.ShapeDtypeStruct(other_terms.shape, jnp.float32),
                pltpu.VMEM((devices, 128), jnp.float32),
            ],
            compiler_params=pltpu.CompilerParams(vmem_limit_bytes=4 << 20),
        )(*parts, other_terms, virtual_sum, occupied)
        squares = lax.all_to_all(squares, AXES, 0, 0, tiled=True)
        update_norm = pl.pallas_call(
            functools.partial(norm_kernel, rows * width),
            out_shape=jax.ShapeDtypeStruct((1, 1), jnp.float32),
            compiler_params=pltpu.CompilerParams(vmem_limit_bytes=4 << 20),
        )(squares).reshape(())
    else:
        ladder = plain_ladder(tile_block, amp_rows, tile_count)
        update = (ladder + other_terms) / (occupied - virtual_sum)
        update_norm = jnp.sqrt(lax.psum(jnp.sum(update * update), AXES) / (rows * width))
    return (update, update_norm)


def solution(mesh):
    in_specs = (P(AXES, None, None, None), P(AXES, None, None, None), P(AXES), P(AXES, None), P(), P(), P(AXES, None))
    out_specs = (P(AXES, None), P())
    body = functools.partial(shards, mesh.shape["wide"], mesh.shape["narrow"])
    return jax.shard_map(body, mesh=mesh, in_specs=in_specs, out_specs=out_specs, check_vma=False)
```

```python
import functools
import jax
import jax.numpy as jnp
from jax import lax
from jax.experimental import pallas as pl
from jax.experimental.pallas import tpu as pltpu
from jax.sharding import PartitionSpec as P

AXES = ("wide", "narrow")
ROW_CHUNK = 256
FAR_ROUTES = ((0, 1), (1, 0))
NEAR_ROUTES = ((2, 1, 0), (1, 0, 2))


def position(order, wide_index):
    spot = wide_index * 0
    for bit in order:
        spot = spot * 2 + ((wide_index >> bit) & 1)
    return spot


def ladder_kernel(block_rows, planes, place_ref, count_ref, tiles_ref, amps_ref, out_ref, tile_buf, amp_buf, tile_sem, amp_sem):
    slots, _, rows = tile_buf.shape
    live = count_ref[0]
    wide_me, narrow_me = place_ref[0], place_ref[1]

    def copies(slot):
        return (
            pltpu.make_async_copy(amps_ref.at[slot], amp_buf.at[slot], amp_sem.at[slot]),
            pltpu.make_async_copy(tiles_ref.at[slot], tile_buf.at[slot], tile_sem.at[slot]),
        )

    for slot in range(slots):

        def load_slot(slot=slot):
            for copy in copies(slot):
                copy.start()

        pl.when(slot < live)(load_slot)

    def spot_of(wide_index, narrow):
        apart = wide_me ^ wide_index
        cross = narrow_me ^ narrow
        plane = apart >> 2
        first, second, third = NEAR_ROUTES[narrow]
        far_spot = plane * 8 + cross * 4 + position(FAR_ROUTES[narrow], apart)
        near_spot = (plane >> 1) * 16 + position((third,), apart) * 8 + cross * 4 + position((first, second), apart)
        return jnp.where(plane >= planes // 2, far_spot, near_spot)

    def add_slots(members, fresh):
        for slot in members:
            for copy in copies(slot):
                copy.wait()
        amps = jnp.concatenate([amp_buf[slot] for slot in members], 0)
        for start in range(0, rows, ROW_CHUNK):
            tiles = jnp.concatenate([tile_buf[slot, :, start : start + ROW_CHUNK] for slot in members], 0)
            term = lax.dot_general(tiles, amps, (((0,), (0,)), ((), ())), preferred_element_type=jnp.float32)
            for offset in range(0, ROW_CHUNK, block_rows):
                wide, narrow = divmod((start + offset) // block_rows, 2)
                spot = spot_of(wide, narrow)
                where = pl.ds(pl.multiple_of(spot * block_rows, block_rows), block_rows)
                block = term[offset : offset + block_rows]
                out_ref[where, :] = block if fresh else out_ref[where, :] + block

    for first in range(0, slots, 2):
        alone = (live == first + 1) if first + 1 < slots else (live > first)
        pl.when(alone)(functools.partial(add_slots, [first], first == 0))
        if first + 1 < slots:
            pl.when(live > first + 1)(functools.partial(add_slots, [first, first + 1], first == 0))


def update_kernel(count, *refs):
    parts = refs[:count]
    other_ref, energy_ref, occupied_ref, update_ref, square_ref = refs[count:]
    ladder = parts[0][...]
    for part in parts[1:]:
        ladder += part[...]
    update = (ladder + other_ref[...]) / (occupied_ref[...] - energy_ref[...])
    update_ref[...] = update
    square_ref[...] = jnp.full(square_ref.shape, jnp.sum(update * update))


def norm_kernel(entries, squares_ref, update_ref, norm_ref, out_ref):
    out_ref[...] = update_ref[...]
    total = jnp.sum(squares_ref[...], axis=0, keepdims=True)
    norm_ref[...] = jnp.sqrt(total / entries)[:, :1]


def flip(value, devices, masks):
    pairs = [(i, i ^ (2 * masks[i % 2])) for i in range(devices)]
    return lax.ppermute(value, AXES, pairs)


def fast_ladder(tile_block, amp_rows, tile_count, wide, narrow):
    slots, depth, rows = tile_block.shape
    width = amp_rows.shape[2]
    devices = wide * narrow
    block_rows = rows // devices
    place = jnp.stack([lax.axis_index("wide"), lax.axis_index("narrow")]).astype(jnp.int32)
    partial = pl.pallas_call(
        functools.partial(ladder_kernel, block_rows, wide // 4),
        out_shape=pltpu.VMEM((rows, width), jnp.float32),
        in_specs=[pl.BlockSpec(memory_space=pltpu.SMEM)] * 2 + [pl.BlockSpec(memory_space=pltpu.HBM)] * 2,
        out_specs=pl.BlockSpec(memory_space=pltpu.VMEM),
        scratch_shapes=[
            pltpu.VMEM((slots, depth, rows), tile_block.dtype),
            pltpu.VMEM((slots, depth, width), amp_rows.dtype),
            pltpu.SemaphoreType.DMA((slots,)),
            pltpu.SemaphoreType.DMA((slots,)),
        ],
        compiler_params=pltpu.CompilerParams(vmem_limit_bytes=32 << 20),
    )(
        place,
        tile_count,
        pltpu.with_memory_space_constraint(tile_block, pltpu.HBM),
        pltpu.with_memory_space_constraint(amp_rows, pltpu.HBM),
    )
    far = wide // 4
    partial = partial.reshape(far, 2, 4, block_rows, width)
    swap = [(i, i ^ 1) for i in range(devices)]
    groups = [range(far // 2), range(far // 2, far)]
    pieces = [partial[g.start : g.stop] for g in groups]
    pieces = [s[:, 0] + lax.ppermute(s[:, 1], AXES, swap) for s in pieces]
    for step in range(2):
        half = 2 >> step
        masks = [[1 << route[step] for route in routes] for routes in (NEAR_ROUTES, FAR_ROUTES)]
        pieces = [s[:, :half] + flip(s[:, half:], devices, mask) for s, mask in zip(pieces, masks)]
    parts = []
    for g, s in zip(groups, pieces):
        for spot in g:
            block = s[spot - g.start, 0]
            masks = [4 * spot] * 2
            if spot < far // 2:
                masks = [(4 * spot & ~4) | ((spot & 1) << route[2]) for route in NEAR_ROUTES]
            parts.append(flip(block, devices, masks) if spot else block)
    return parts


def plain_ladder(tile_block, amp_rows, tile_count):
    slots, depth, rows = tile_block.shape
    live = lax.broadcasted_iota(jnp.int32, (slots, 1, 1), 0) < tile_count[0]
    amps = jnp.where(live, amp_rows, jnp.zeros_like(amp_rows))
    partial = lax.dot_general(
        tile_block.reshape(slots * depth, rows),
        amps.reshape(slots * depth, amp_rows.shape[2]),
        (((0,), (0,)), ((), ())),
        preferred_element_type=jnp.float32,
    )
    partial = lax.psum_scatter(partial, "wide", scatter_dimension=0, tiled=True)
    return lax.psum_scatter(partial, "narrow", scatter_dimension=0, tiled=True)


def shards(wide, narrow, integrals, amplitudes, tile_count, row_orbitals, virtual_energy, occupied_energy, other_terms):
    tile_block = integrals[0]
    amp_rows = amplitudes[0]
    rows = tile_block.shape[2]
    width = amp_rows.shape[2]
    devices = wide * narrow
    fast = narrow == 2 and wide >= 16 and wide & (wide - 1) == 0 and rows % (16 * devices) == 0 and width % 512 == 0
    orbital_ids = lax.broadcasted_iota(jnp.int32, (1, virtual_energy.shape[0]), 1)
    energy_row = virtual_energy[None, :]
    first_energy = jnp.sum(jnp.where(row_orbitals[:, 0:1] == orbital_ids, energy_row, 0.0), axis=1)
    second_energy = jnp.sum(jnp.where(row_orbitals[:, 1:2] == orbital_ids, energy_row, 0.0), axis=1)
    virtual_sum = (first_energy + second_energy)[:, None]
    occupied = occupied_energy[None, :]
    if fast:
        parts = fast_ladder(tile_block, amp_rows, tile_count, wide, narrow)
        update, squares = pl.pallas_call(
            functools.partial(update_kernel, len(parts)),
            out_shape=[
                pltpu.VMEM(other_terms.shape, jnp.float32),
                pltpu.VMEM((devices, 128), jnp.float32),
            ],
            compiler_params=pltpu.CompilerParams(vmem_limit_bytes=4 << 20),
        )(*parts, other_terms, virtual_sum, occupied)
        squares = lax.all_to_all(squares, AXES, 0, 0, tiled=True)
        update_norm, update = pl.pallas_call(
            functools.partial(norm_kernel, rows * width),
            out_shape=[
                jax.ShapeDtypeStruct((1, 1), jnp.float32),
                jax.ShapeDtypeStruct(other_terms.shape, jnp.float32),
            ],
            compiler_params=pltpu.CompilerParams(vmem_limit_bytes=4 << 20),
        )(squares, update)
        update_norm = update_norm.reshape(())
    else:
        ladder = plain_ladder(tile_block, amp_rows, tile_count)
        update = (ladder + other_terms) / (occupied - virtual_sum)
        update_norm = jnp.sqrt(lax.psum(jnp.sum(update * update), AXES) / (rows * width))
    return (update, update_norm)


def solution(mesh):
    in_specs = (P(AXES, None, None, None), P(AXES, None, None, None), P(AXES), P(AXES, None), P(), P(), P(AXES, None))
    out_specs = (P(AXES, None), P())
    body = functools.partial(shards, mesh.shape["wide"], mesh.shape["narrow"])
    return jax.shard_map(body, mesh=mesh, in_specs=in_specs, out_specs=out_specs, check_vma=False)
```

```python
import functools
import jax
import jax.numpy as jnp
from jax import lax
from jax.experimental import pallas as pl
from jax.experimental.pallas import tpu as pltpu
from jax.sharding import PartitionSpec as P

AXES = ("wide", "narrow")
ROW_CHUNK = 256
FAR_ROUTES = ((0, 1), (1, 0))
NEAR_ROUTES = ((2, 1, 0), (1, 0, 2))


def position(order, wide_index):
    spot = wide_index * 0
    for bit in order:
        spot = spot * 2 + ((wide_index >> bit) & 1)
    return spot


def ladder_kernel(block_rows, planes, count_ref, tiles_ref, amps_ref, out_ref, tile_buf, amp_buf, tile_sem, amp_sem):
    slots, _, rows = tile_buf.shape
    live = count_ref[0]
    wide_me, narrow_me = lax.axis_index("wide"), lax.axis_index("narrow")

    def copies(slot):
        return (
            pltpu.make_async_copy(amps_ref.at[slot], amp_buf.at[slot], amp_sem.at[slot]),
            pltpu.make_async_copy(tiles_ref.at[slot], tile_buf.at[slot], tile_sem.at[slot]),
        )

    for slot in range(slots):

        def load_slot(slot=slot):
            for copy in copies(slot):
                copy.start()

        pl.when(slot < live)(load_slot)

    def spot_of(wide_index, narrow):
        apart = wide_me ^ wide_index
        cross = narrow_me ^ narrow
        plane = apart >> 2
        first, second, third = NEAR_ROUTES[narrow]
        far_spot = plane * 8 + cross * 4 + position(FAR_ROUTES[narrow], apart)
        near_spot = (plane >> 1) * 16 + position((third,), apart) * 8 + cross * 4 + position((first, second), apart)
        return jnp.where(plane >= planes // 2, far_spot, near_spot)

    def add_slots(members, fresh):
        for slot in members:
            for copy in copies(slot):
                copy.wait()
        amps = jnp.concatenate([amp_buf[slot] for slot in members], 0)
        for start in range(0, rows, ROW_CHUNK):
            tiles = jnp.concatenate([tile_buf[slot, :, start : start + ROW_CHUNK] for slot in members], 0)
            term = lax.dot_general(tiles, amps, (((0,), (0,)), ((), ())), preferred_element_type=jnp.float32)
            for offset in range(0, ROW_CHUNK, block_rows):
                wide, narrow = divmod((start + offset) // block_rows, 2)
                spot = spot_of(wide, narrow)
                where = pl.ds(pl.multiple_of(spot * block_rows, block_rows), block_rows)
                block = term[offset : offset + block_rows]
                out_ref[where, :] = block if fresh else out_ref[where, :] + block

    for first in range(0, slots, 2):
        alone = (live == first + 1) if first + 1 < slots else (live > first)
        pl.when(alone)(functools.partial(add_slots, [first], first == 0))
        if first + 1 < slots:
            pl.when(live > first + 1)(functools.partial(add_slots, [first, first + 1], first == 0))


def update_kernel(count, *refs):
    parts = refs[:count]
    other_ref, energy_ref, occupied_ref, update_ref, square_ref = refs[count:]
    ladder = parts[0][...]
    for part in parts[1:]:
        ladder += part[...]
    update = (ladder + other_ref[...]) / (occupied_ref[...] - energy_ref[...])
    update_ref[...] = update
    square_ref[...] = jnp.full(square_ref.shape, jnp.sum(update * update))


def norm_kernel(entries, squares_ref, update_ref, norm_ref, out_ref):
    out_ref[...] = update_ref[...]
    total = jnp.sum(squares_ref[...], axis=0, keepdims=True)
    norm_ref[...] = jnp.sqrt(total / entries)[:, :1]


def flip(value, devices, masks):
    pairs = [(i, i ^ (2 * masks[i % 2])) for i in range(devices)]
    return lax.ppermute(value, AXES, pairs)


def fast_ladder(tile_block, amp_rows, tile_count, wide, narrow):
    slots, depth, rows = tile_block.shape
    width = amp_rows.shape[2]
    devices = wide * narrow
    block_rows = rows // devices
    partial = pl.pallas_call(
        functools.partial(ladder_kernel, block_rows, wide // 4),
        out_shape=pltpu.VMEM((rows, width), jnp.float32),
        in_specs=[pl.BlockSpec(memory_space=pltpu.SMEM)] + [pl.BlockSpec(memory_space=pltpu.HBM)] * 2,
        out_specs=pl.BlockSpec(memory_space=pltpu.VMEM),
        scratch_shapes=[
            pltpu.VMEM((slots, depth, rows), tile_block.dtype),
            pltpu.VMEM((slots, depth, width), amp_rows.dtype),
            pltpu.SemaphoreType.DMA((slots,)),
            pltpu.SemaphoreType.DMA((slots,)),
        ],
        compiler_params=pltpu.CompilerParams(vmem_limit_bytes=32 << 20),
    )(
        tile_count,
        pltpu.with_memory_space_constraint(tile_block, pltpu.HBM),
        pltpu.with_memory_space_constraint(amp_rows, pltpu.HBM),
    )
    far = wide // 4
    partial = partial.reshape(far, 2, 4, block_rows, width)
    swap = [(i, i ^ 1) for i in range(devices)]
    groups = [range(far // 2), range(far // 2, far)]
    pieces = [partial[g.start : g.stop] for g in groups]
    pieces = [s[:, 0] + lax.ppermute(s[:, 1], AXES, swap) for s in pieces]
    for step in range(2):
        half = 2 >> step
        masks = [[1 << route[step] for route in routes] for routes in (NEAR_ROUTES, FAR_ROUTES)]
        pieces = [s[:, :half] + flip(s[:, half:], devices, mask) for s, mask in zip(pieces, masks)]
    parts = []
    for g, s in zip(groups, pieces):
        for spot in g:
            block = s[spot - g.start, 0]
            masks = [4 * spot] * 2
            if spot < far // 2:
                masks = [(4 * spot & ~4) | ((spot & 1) << route[2]) for route in NEAR_ROUTES]
            parts.append(flip(block, devices, masks) if spot else block)
    return parts


def plain_ladder(tile_block, amp_rows, tile_count):
    slots, depth, rows = tile_block.shape
    live = lax.broadcasted_iota(jnp.int32, (slots, 1, 1), 0) < tile_count[0]
    amps = jnp.where(live, amp_rows, jnp.zeros_like(amp_rows))
    partial = lax.dot_general(
        tile_block.reshape(slots * depth, rows),
        amps.reshape(slots * depth, amp_rows.shape[2]),
        (((0,), (0,)), ((), ())),
        preferred_element_type=jnp.float32,
    )
    partial = lax.psum_scatter(partial, "wide", scatter_dimension=0, tiled=True)
    return lax.psum_scatter(partial, "narrow", scatter_dimension=0, tiled=True)


def shards(wide, narrow, integrals, amplitudes, tile_count, row_orbitals, virtual_energy, occupied_energy, other_terms):
    tile_block = integrals[0]
    amp_rows = amplitudes[0]
    rows = tile_block.shape[2]
    width = amp_rows.shape[2]
    devices = wide * narrow
    fast = narrow == 2 and wide >= 16 and wide & (wide - 1) == 0 and rows % (16 * devices) == 0 and width % 512 == 0
    orbital_ids = lax.broadcasted_iota(jnp.int32, (1, virtual_energy.shape[0]), 1)
    energy_row = virtual_energy[None, :]
    first_energy = jnp.sum(jnp.where(row_orbitals[:, 0:1] == orbital_ids, energy_row, 0.0), axis=1)
    second_energy = jnp.sum(jnp.where(row_orbitals[:, 1:2] == orbital_ids, energy_row, 0.0), axis=1)
    virtual_sum = (first_energy + second_energy)[:, None]
    occupied = occupied_energy[None, :]
    if fast:
        parts = fast_ladder(tile_block, amp_rows, tile_count, wide, narrow)
        update, squares = pl.pallas_call(
            functools.partial(update_kernel, len(parts)),
            out_shape=[
                pltpu.VMEM(other_terms.shape, jnp.float32),
                pltpu.VMEM((devices, 128), jnp.float32),
            ],
            compiler_params=pltpu.CompilerParams(vmem_limit_bytes=4 << 20),
        )(*parts, other_terms, virtual_sum, occupied)
        squares = lax.all_to_all(squares, AXES, 0, 0, tiled=True)
        update_norm, update = pl.pallas_call(
            functools.partial(norm_kernel, rows * width),
            out_shape=[
                jax.ShapeDtypeStruct((1, 1), jnp.float32),
                jax.ShapeDtypeStruct(other_terms.shape, jnp.float32),
            ],
            compiler_params=pltpu.CompilerParams(vmem_limit_bytes=4 << 20),
        )(squares, update)
        update_norm = update_norm.reshape(())
    else:
        ladder = plain_ladder(tile_block, amp_rows, tile_count)
        update = (ladder + other_terms) / (occupied - virtual_sum)
        update_norm = jnp.sqrt(lax.psum(jnp.sum(update * update), AXES) / (rows * width))
    return (update, update_norm)


def solution(mesh):
    in_specs = (P(AXES, None, None, None), P(AXES, None, None, None), P(AXES), P(AXES, None), P(), P(), P(AXES, None))
    out_specs = (P(AXES, None), P())
    body = functools.partial(shards, mesh.shape["wide"], mesh.shape["narrow"])
    return jax.shard_map(body, mesh=mesh, in_specs=in_specs, out_specs=out_specs, check_vma=False)
```

```python
import functools
import jax
import jax.numpy as jnp
from jax import lax
from jax.experimental import pallas as pl
from jax.experimental.pallas import tpu as pltpu
from jax.sharding import PartitionSpec as P

AXES = ("wide", "narrow")
ROW_CHUNK = 256
FAR_ROUTES = ((0, 1), (1, 0))
NEAR_ROUTES = ((2, 1, 0), (1, 0, 2))


def position(order, wide_index):
    spot = wide_index * 0
    for bit in order:
        spot = spot * 2 + ((wide_index >> bit) & 1)
    return spot


def ladder_kernel(block_rows, planes, count_ref, tiles_ref, amps_ref, out_ref, tile_buf, amp_buf, tile_sem, amp_sem):
    slots, _, rows = tile_buf.shape
    live = count_ref[0]
    wide_me, narrow_me = lax.axis_index("wide"), lax.axis_index("narrow")

    def copies(slot):
        return (
            pltpu.make_async_copy(amps_ref.at[slot], amp_buf.at[slot], amp_sem.at[slot]),
            pltpu.make_async_copy(tiles_ref.at[slot], tile_buf.at[slot], tile_sem.at[slot]),
        )

    for slot in range(slots):

        def load_slot(slot=slot):
            for copy in copies(slot):
                copy.start()

        pl.when(slot < live)(load_slot)

    def spot_of(wide_index, narrow):
        apart = wide_me ^ wide_index
        cross = narrow_me ^ narrow
        plane = apart >> 2
        first, second, third = NEAR_ROUTES[narrow]
        far_spot = plane * 8 + cross * 4 + position(FAR_ROUTES[narrow], apart)
        near_spot = (plane >> 1) * 16 + position((third,), apart) * 8 + cross * 4 + position((first, second), apart)
        return jnp.where(plane >= planes // 2, far_spot, near_spot)

    def add_slots(members, fresh):
        for slot in members:
            for copy in copies(slot):
                copy.wait()
        amps = jnp.concatenate([amp_buf[slot] for slot in members], 0)
        for start in range(0, rows, ROW_CHUNK):
            tiles = jnp.concatenate([tile_buf[slot, :, start : start + ROW_CHUNK] for slot in members], 0)
            term = lax.dot_general(tiles, amps, (((0,), (0,)), ((), ())), preferred_element_type=jnp.float32)
            for offset in range(0, ROW_CHUNK, block_rows):
                wide, narrow = divmod((start + offset) // block_rows, 2)
                spot = spot_of(wide, narrow)
                where = pl.ds(pl.multiple_of(spot * block_rows, block_rows), block_rows)
                block = term[offset : offset + block_rows]
                out_ref[where, :] = block if fresh else out_ref[where, :] + block

    for first in range(0, slots, 2):
        alone = (live == first + 1) if first + 1 < slots else (live > first)
        pl.when(alone)(functools.partial(add_slots, [first], first == 0))
        if first + 1 < slots:
            pl.when(live > first + 1)(functools.partial(add_slots, [first, first + 1], first == 0))


def update_kernel(count, *refs):
    parts = refs[:count]
    other_ref, energy_ref, occupied_ref, update_ref, square_ref = refs[count:]
    ladder = parts[0][...]
    for part in parts[1:]:
        ladder += part[...]
    update = (ladder + other_ref[...]) / (occupied_ref[...] - energy_ref[...])
    update_ref[...] = update
    square_ref[...] = jnp.full(square_ref.shape, jnp.sum(update * update))


def norm_kernel(entries, squares_ref, update_ref, norm_ref, out_ref, out_sem):
    copy = pltpu.make_async_copy(update_ref, out_ref, out_sem)
    copy.start()
    total = jnp.sum(squares_ref[...], axis=0, keepdims=True)
    norm_ref[...] = jnp.sqrt(total / entries)[:, :1]
    copy.wait()


def flip(value, devices, masks):
    pairs = [(i, i ^ (2 * masks[i % 2])) for i in range(devices)]
    return lax.ppermute(value, AXES, pairs)


def fast_ladder(tile_block, amp_rows, tile_count, wide, narrow):
    slots, depth, rows = tile_block.shape
    width = amp_rows.shape[2]
    devices = wide * narrow
    block_rows = rows // devices
    partial = pl.pallas_call(
        functools.partial(ladder_kernel, block_rows, wide // 4),
        out_shape=pltpu.VMEM((rows, width), jnp.float32),
        in_specs=[pl.BlockSpec(memory_space=pltpu.SMEM)] + [pl.BlockSpec(memory_space=pltpu.HBM)] * 2,
        out_specs=pl.BlockSpec(memory_space=pltpu.VMEM),
        scratch_shapes=[
            pltpu.VMEM((slots, depth, rows), tile_block.dtype),
            pltpu.VMEM((slots, depth, width), amp_rows.dtype),
            pltpu.SemaphoreType.DMA((slots,)),
            pltpu.SemaphoreType.DMA((slots,)),
        ],
        compiler_params=pltpu.CompilerParams(vmem_limit_bytes=32 << 20),
    )(
        tile_count,
        pltpu.with_memory_space_constraint(tile_block, pltpu.HBM),
        pltpu.with_memory_space_constraint(amp_rows, pltpu.HBM),
    )
    far = wide // 4
    partial = partial.reshape(far, 2, 4, block_rows, width)
    swap = [(i, i ^ 1) for i in range(devices)]
    groups = [range(far // 2), range(far // 2, far)]
    pieces = [partial[g.start : g.stop] for g in groups]
    pieces = [s[:, 0] + lax.ppermute(s[:, 1], AXES, swap) for s in pieces]
    for step in range(2):
        half = 2 >> step
        masks = [[1 << route[step] for route in routes] for routes in (NEAR_ROUTES, FAR_ROUTES)]
        pieces = [s[:, :half] + flip(s[:, half:], devices, mask) for s, mask in zip(pieces, masks)]
    parts = []
    for g, s in zip(groups, pieces):
        for spot in g:
            block = s[spot - g.start, 0]
            masks = [4 * spot] * 2
            if spot < far // 2:
                masks = [(4 * spot & ~4) | ((spot & 1) << route[2]) for route in NEAR_ROUTES]
            parts.append(flip(block, devices, masks) if spot else block)
    return parts


def plain_ladder(tile_block, amp_rows, tile_count):
    slots, depth, rows = tile_block.shape
    live = lax.broadcasted_iota(jnp.int32, (slots, 1, 1), 0) < tile_count[0]
    amps = jnp.where(live, amp_rows, jnp.zeros_like(amp_rows))
    partial = lax.dot_general(
        tile_block.reshape(slots * depth, rows),
        amps.reshape(slots * depth, amp_rows.shape[2]),
        (((0,), (0,)), ((), ())),
        preferred_element_type=jnp.float32,
    )
    partial = lax.psum_scatter(partial, "wide", scatter_dimension=0, tiled=True)
    return lax.psum_scatter(partial, "narrow", scatter_dimension=0, tiled=True)


def shards(wide, narrow, integrals, amplitudes, tile_count, row_orbitals, virtual_energy, occupied_energy, other_terms):
    tile_block = integrals[0]
    amp_rows = amplitudes[0]
    rows = tile_block.shape[2]
    width = amp_rows.shape[2]
    devices = wide * narrow
    fast = narrow == 2 and wide >= 16 and wide & (wide - 1) == 0 and rows % (16 * devices) == 0 and width % 512 == 0
    orbital_ids = lax.broadcasted_iota(jnp.int32, (1, virtual_energy.shape[0]), 1)
    energy_row = virtual_energy[None, :]
    first_energy = jnp.sum(jnp.where(row_orbitals[:, 0:1] == orbital_ids, energy_row, 0.0), axis=1)
    second_energy = jnp.sum(jnp.where(row_orbitals[:, 1:2] == orbital_ids, energy_row, 0.0), axis=1)
    virtual_sum = (first_energy + second_energy)[:, None]
    occupied = occupied_energy[None, :]
    if fast:
        parts = fast_ladder(tile_block, amp_rows, tile_count, wide, narrow)
        update, squares = pl.pallas_call(
            functools.partial(update_kernel, len(parts)),
            out_shape=[
                pltpu.VMEM(other_terms.shape, jnp.float32),
                pltpu.VMEM((devices, 128), jnp.float32),
            ],
            compiler_params=pltpu.CompilerParams(vmem_limit_bytes=4 << 20),
        )(*parts, other_terms, virtual_sum, occupied)
        squares = lax.all_to_all(squares, AXES, 0, 0, tiled=True)
        update_norm, update = pl.pallas_call(
            functools.partial(norm_kernel, rows * width),
            out_shape=[
                jax.ShapeDtypeStruct((1, 1), jnp.float32),
                jax.ShapeDtypeStruct(other_terms.shape, jnp.float32),
            ],
            out_specs=[pl.BlockSpec(memory_space=pltpu.VMEM), pl.BlockSpec(memory_space=pltpu.HBM)],
            scratch_shapes=[pltpu.SemaphoreType.DMA],
            compiler_params=pltpu.CompilerParams(vmem_limit_bytes=4 << 20),
        )(squares, update)
        update_norm = update_norm.reshape(())
    else:
        ladder = plain_ladder(tile_block, amp_rows, tile_count)
        update = (ladder + other_terms) / (occupied - virtual_sum)
        update_norm = jnp.sqrt(lax.psum(jnp.sum(update * update), AXES) / (rows * width))
    return (update, update_norm)


def solution(mesh):
    in_specs = (P(AXES, None, None, None), P(AXES, None, None, None), P(AXES), P(AXES, None), P(), P(), P(AXES, None))
    out_specs = (P(AXES, None), P())
    body = functools.partial(shards, mesh.shape["wide"], mesh.shape["narrow"])
    return jax.shard_map(body, mesh=mesh, in_specs=in_specs, out_specs=out_specs, check_vma=False)
```
